256 devices in a mesh: pipe: 8 (over y_lo, x), expert: 32 (over y_hi, z, core).
Axes of the slice: x: 4, y: 4 (y_hi: 2, y_lo: 2; y = y_hi * 2 + y_lo), z: 8, core: 2. Of those that a mesh axis runs over, the one named last changes fastest.
Arguments:
- x_fwd: bfloat16 [8, 2048, 3584], P('pipe', 'expert'), may hold values from -6 to 6
- routes_fwd: int32 [8, 2048, 1], P('pipe', 'expert'), may hold values from 0 to 7; in each aligned block of 64 rows (0 to 63, 64 to 127, ..., all dimensions but the last counted through in order) at most 12 rows name the same one
- gates_fwd: float32 [8, 2048, 1], P('pipe', 'expert'), may hold values from 0.25 to 1.5
- x_bwd: bfloat16 [8, 2048, 3584], P('pipe', 'expert'), may hold values from -6 to 6
- grad_bwd: bfloat16 [8, 2048, 3584], P('pipe', 'expert'), may hold values from -6 to 6
- routes_bwd: int32 [8, 2048, 1], P('pipe', 'expert'), may hold values from 0 to 7; in each aligned block of 64 rows (0 to 63, 64 to 127, ..., all dimensions but the last counted through in order) at most 12 rows name the same one
- gates_bwd: float32 [8, 2048, 1], P('pipe', 'expert'), may hold values from 0.25 to 1.5
- gate_proj: bfloat16 [8, 3584, 8192], P('pipe', None, 'expert'), may hold values from -0.09375 to 0.09375
- up_proj: bfloat16 [8, 3584, 8192], P('pipe', None, 'expert'), may hold values from -0.09375 to 0.09375
- down_proj: bfloat16 [8, 8192, 3584], P('pipe', 'expert'), may hold values from -0.1875 to 0.1875
Outputs:
- fwd_next: bfloat16 [8, 2048, 3584], P('pipe', 'expert')
- bwd_next: bfloat16 [8, 2048, 3584], P('pipe', 'expert')
The draws below stay inside these ranges and needn't reach their ends.
Inputs may be any that keep to these rules, and one draw needn't show every extreme that they name: `routes_fwd`: each token names 1 different experts. Among the 64 tokens of one device no expert is named more than 12 times, and in every draw some expert is named exactly 12 times by the tokens of one device. `routes_bwd`: as for routes_fwd.
All inputs are finite; a program needn't handle non-finite values.
Results may differ from the reference program's by a relative error of at most 0.007.
Values may be sent and summed in bfloat16 or wider, within the bound.
No kernel may reach another device: no remote copies, remote signals or barrier semaphores. Data moves between devices by JAX's collectives and lax.ppermute only.
A program may use at most 128 MiB of HBM per device.

```python
import math
import jax
import jax.numpy as jnp
import numpy as np
from jax import lax

D = 3584
FF = 1024
HSPLIT = 4
TOPK = 1
TOK_DEV = 64
EXPERTS = 8
CAP = 12
TOKENS = 2048
N_PIPE = 8
N_EXPERT = 32


def steps_of(key, shape, cuts, smallest, largest):
    loudness, own = 1.0, jax.random.fold_in(key, 6)
    for axis_at, shards_of in cuts:
        draws = jnp.exp(jax.random.uniform(jax.random.fold_in(own, axis_at), (shards_of,), jnp.float32, smallest / len(cuts), largest / len(cuts)))
        loudness = loudness * jnp.repeat(draws, shape[axis_at] // shards_of).reshape([-1 if axis == axis_at else 1 for axis in range(len(shape))])
    return loudness


def routed_block(stream_key, own, number, rows, number_of, top, most, lean):
    ranking = jax.random.permutation(stream_key, number_of)
    packed, usual = portions_of(number_of, rows * top, most, lean, True), portions_of(number_of, rows * top, most, lean, False)
    places = jnp.arange(number_of)

    def named(lengths, turn):
        used = int((lengths > 0).sum())
        fixed = max(1, used // 4)
        passed = fixed + (places - fixed + turn * (used - fixed)) % max(1, number_of - fixed)
        return jnp.zeros((number_of,), jnp.int32).at[ranking[jnp.where(places < fixed, places, passed)]].set(jnp.asarray(lengths, jnp.int32))

    lengths = jnp.where(number % 4 == 0, named(packed, number // 4), named(usual, number - number // 4 - 1))
    mixed = jax.random.permutation(jax.random.fold_in(own, 3), number_of)
    source_of, taker = mixed[0:number_of // 2 * 2:2], mixed[1:number_of // 2 * 2:2]
    margin = jnp.minimum(lengths[source_of] - 1, most - lengths[taker]) // 2
    margin = jnp.where((source_of == ranking[0]) | (taker == ranking[0]) | (lengths[taker] == 0), 0, jnp.maximum(margin, 0))
    passed = jax.random.randint(jax.random.fold_in(own, 4), (number_of // 2,), 0, 1 << 20) % (margin + 1)
    lengths = lengths.at[source_of].add(-passed).at[taker].add(passed)
    items = jnp.searchsorted(jnp.cumsum(lengths), jnp.arange(rows * top), side="right").astype(jnp.int32)
    listing = items.reshape(top, rows).T
    listing = listing[jax.random.permutation(jax.random.fold_in(own, 1), rows)]
    turn = jax.random.randint(jax.random.fold_in(own, 2), (rows, 1), 0, top)
    return jnp.take_along_axis(listing, (jnp.arange(top)[None, :] + turn) % top, axis=1)


def portions_of(number_of, total, bound, slope, full):
    portions = [(1 << 20) // math.isqrt(grade ** slope) + 1 for grade in range(1, number_of + 1)]
    largest = bound if full else min(bound, max(-(-total // number_of), total * portions[0] // sum(portions)))
    least = 1 if total - largest >= number_of - 1 else 0
    given, spare = [largest] + [least] * (number_of - 1), total - largest - least * (number_of - 1)
    while spare > 0:
        candidates = [i for i in range(1, number_of) if given[i] < largest] or [i for i in range(1, number_of) if given[i] < bound]
        pool, left = sum([portions[i] for i in candidates]), spare
        for i in candidates:
            extra = min(bound - given[i], max(1, left * portions[i] // pool), spare)
            given[i] = given[i] + extra
            spare = spare - extra
    return np.array(given)


def normal_values(stream_key, shape, scale, reach, shards=(), kind=jnp.bfloat16):
    gain = steps_of(stream_key, shape, shards, -0.22, 0.18) if shards else 1.0
    values = jax.random.normal(stream_key, shape, jnp.float32) * scale * gain
    return jnp.minimum(jnp.maximum(values, -reach), reach).astype(kind)


def setup_inputs(seed: int = 0) -> dict:
    key_of = jax.random.split(jax.random.key(seed), 11)
    x_fwd = normal_values(key_of[0], (N_PIPE, TOKENS, D), 1.0, 6.0, ((0, 8), (1, 32)))
    routes_fwd_keys = jax.random.split(jax.random.fold_in(key_of[1], 1), N_PIPE * TOKENS // TOK_DEV)
    routes_fwd_turns = jax.random.permutation(jax.random.fold_in(key_of[1], 3), N_PIPE * TOKENS // TOK_DEV)
    routes_fwd = jax.vmap(lambda own, number: routed_block(jax.random.fold_in(key_of[1], 2), own, number, TOK_DEV, EXPERTS, TOPK, CAP, 1))(routes_fwd_keys, routes_fwd_turns).reshape((N_PIPE, TOKENS, TOPK))
    gates_fwd = jnp.clip(0.25 + 1.25 * jax.random.uniform(key_of[2], (N_PIPE, TOKENS, TOPK), jnp.float32) ** steps_of(key_of[2], (N_PIPE, TOKENS, TOPK), ((0, 8), (1, 32)), -0.2, 0.2), 0.25, 1.5)
    x_bwd = normal_values(key_of[3], (N_PIPE, TOKENS, D), 1.0, 6.0, ((0, 8), (1, 32)))
    grad_bwd = normal_values(key_of[4], (N_PIPE, TOKENS, D), 1.0, 6.0, ((0, 8), (1, 32)))
    routes_bwd_keys = jax.random.split(jax.random.fold_in(key_of[5], 1), N_PIPE * TOKENS // TOK_DEV)
    routes_bwd_turns = jax.random.permutation(jax.random.fold_in(key_of[5], 3), N_PIPE * TOKENS // TOK_DEV)
    routes_bwd = jax.vmap(lambda own, number: routed_block(jax.random.fold_in(key_of[5], 2), own, number, TOK_DEV, EXPERTS, TOPK, CAP, 1))(routes_bwd_keys, routes_bwd_turns).reshape((N_PIPE, TOKENS, TOPK))
    gates_bwd = jnp.clip(0.25 + 1.25 * jax.random.uniform(key_of[6], (N_PIPE, TOKENS, TOPK), jnp.float32) ** steps_of(key_of[6], (N_PIPE, TOKENS, TOPK), ((0, 8), (1, 32)), -0.2, 0.2), 0.25, 1.5)
    gate_proj = normal_values(key_of[7], (N_PIPE, D, EXPERTS * FF), D ** -0.5, 0.09375, ((0, 8), (2, 32)))
    up_proj = normal_values(key_of[8], (N_PIPE, D, EXPERTS * FF), D ** -0.5, 0.09375, ((0, 8), (2, 32)))
    down_proj = normal_values(key_of[9], (N_PIPE, EXPERTS * FF, D), FF ** -0.5, 0.1875, ((0, 8), (1, 32)))
    return {"x_fwd": x_fwd, "routes_fwd": routes_fwd, "gates_fwd": gates_fwd, "x_bwd": x_bwd, "grad_bwd": grad_bwd, "routes_bwd": routes_bwd, "gates_bwd": gates_bwd, "gate_proj": gate_proj, "up_proj": up_proj, "down_proj": down_proj}


def slot_table(routes):
    flat_ids = routes.reshape(-1).astype(jnp.int32)
    hit_table = (flat_ids[:, None] == jnp.arange(EXPERTS, dtype=jnp.int32)[None, :]).astype(jnp.int32)
    earlier = (jnp.cumsum(hit_table, axis=0) - hit_table).astype(jnp.int32)
    places = jnp.sum(earlier * hit_table, axis=1).astype(jnp.int32)
    return places.reshape(routes.shape)


def source_ids(routes):
    return jnp.broadcast_to(jnp.arange(N_EXPERT, dtype=jnp.int32)[:, None, None], routes.shape)


def to_experts(values, routes, places):
    row_block = values.reshape(N_EXPERT, TOK_DEV, 1, D)
    spread = jnp.broadcast_to(row_block, (N_EXPERT, TOK_DEV, TOPK, D))
    buffer = jnp.zeros((EXPERTS, N_EXPERT, CAP, D), values.dtype)
    buffer = buffer.at[routes, source_ids(routes), places].set(spread)
    return buffer.reshape(EXPERTS, N_EXPERT * CAP, D)


def from_experts(base, sums, routes, places, weights):
    sum_table = sums.reshape(EXPERTS, N_EXPERT, CAP, D)
    picked = sum_table[routes, source_ids(routes), places]
    weighted = jnp.sum(weights.reshape(N_EXPERT, TOK_DEV, TOPK, 1) * picked, axis=2)
    return (base.astype(jnp.float32) + weighted.reshape(TOKENS, D)).astype(jnp.bfloat16)


def forward_expert(row_block, gate_cols, up_cols, down_rows):
    pre_gate = jnp.dot(row_block, gate_cols, preferred_element_type=jnp.float32)
    pre_up = jnp.dot(row_block, up_cols, preferred_element_type=jnp.float32)
    hidden = (jax.nn.silu(pre_gate) * pre_up).astype(jnp.bfloat16)
    split_hidden = hidden.astype(jnp.float32).reshape(-1, HSPLIT, FF // HSPLIT)
    split_down = down_rows.astype(jnp.float32).reshape(HSPLIT, FF // HSPLIT, D)
    pieces = jnp.einsum("rsh,shd->srd", split_hidden, split_down).astype(jnp.bfloat16)
    return jnp.sum(pieces.astype(jnp.float32), axis=0)


def backward_expert(rows_x, rows_g, gate_cols, up_cols, down_rows):
    pre_gate = jnp.dot(rows_x, gate_cols, preferred_element_type=jnp.float32)
    pre_up = jnp.dot(rows_x, up_cols, preferred_element_type=jnp.float32)
    act_grad = jnp.dot(rows_g, down_rows.T, preferred_element_type=jnp.float32)
    sigmoid_gate = jax.nn.sigmoid(pre_gate)
    gate_grad = (act_grad * pre_up * sigmoid_gate * (1.0 + pre_gate * (1.0 - sigmoid_gate))).astype(jnp.bfloat16)
    up_grad = (act_grad * pre_gate * sigmoid_gate).astype(jnp.bfloat16)
    split_gate = gate_cols.astype(jnp.float32).reshape(D, HSPLIT, FF // HSPLIT)
    split_up = up_cols.astype(jnp.float32).reshape(D, HSPLIT, FF // HSPLIT)
    pieces = jnp.einsum("rsh,dsh->srd", gate_grad.astype(jnp.float32).reshape(-1, HSPLIT, FF // HSPLIT), split_gate)
    pieces = pieces + jnp.einsum("rsh,dsh->srd", up_grad.astype(jnp.float32).reshape(-1, HSPLIT, FF // HSPLIT), split_up)
    return jnp.sum(pieces.astype(jnp.bfloat16).astype(jnp.float32), axis=0)


def one_section(section_args):
    tokens_a, routes_a, gates_a, tokens_b, grads_b, routes_b, gates_b, gate_section, up_section, down_section = section_args
    gate_all = jnp.moveaxis(gate_section.reshape(D, EXPERTS, FF), 1, 0)
    up_all = jnp.moveaxis(up_section.reshape(D, EXPERTS, FF), 1, 0)
    down_all = down_section.reshape(EXPERTS, FF, D)
    ids_a = routes_a.reshape(N_EXPERT, TOK_DEV, TOPK).astype(jnp.int32)
    ids_b = routes_b.reshape(N_EXPERT, TOK_DEV, TOPK).astype(jnp.int32)
    places_a = jax.vmap(slot_table)(ids_a)
    places_b = jax.vmap(slot_table)(ids_b)
    rows_a = to_experts(tokens_a, ids_a, places_a)
    rows_xb = to_experts(tokens_b, ids_b, places_b)
    rows_gb = to_experts(grads_b, ids_b, places_b)

    def forward_item(item):
        return forward_expert(item[0], item[1], item[2], item[3])

    def backward_item(item):
        return backward_expert(item[0], item[1], item[2], item[3], item[4])

    sums_a = lax.map(forward_item, (rows_a, gate_all, up_all, down_all))
    sums_b = lax.map(backward_item, (rows_xb, rows_gb, gate_all, up_all, down_all))
    out_a = from_experts(tokens_a, sums_a, ids_a, places_a, gates_a)
    out_b = from_experts(grads_b, sums_b, ids_b, places_b, gates_b)
    return out_a, out_b


def reference(x_fwd, routes_fwd, gates_fwd, x_bwd, grad_bwd, routes_bwd, gates_bwd, gate_proj, up_proj, down_proj):
    outs_a, outs_b = lax.map(one_section, (x_fwd, routes_fwd, gates_fwd, x_bwd, grad_bwd, routes_bwd, gates_bwd, gate_proj, up_proj, down_proj))
    fwd_next = jnp.concatenate([jnp.zeros_like(outs_a[:1]), outs_a[:-1]], axis=0)
    bwd_next = jnp.concatenate([outs_b[1:], jnp.zeros_like(outs_b[:1])], axis=0)
    return fwd_next, bwd_next
```

```python
import jax
import jax.numpy as jnp
from jax import lax
from jax.sharding import PartitionSpec as P

HSPLIT = 4
TOPK = 1


def shifted(block, axis, distance):
    devices = range(lax.axis_size(axis))
    route = [(i - distance, i) for i in devices if i - distance in devices]
    return lax.ppermute(block, axis, route)


def slot_table(routes, experts, capacity):
    flat_ids = routes.reshape(-1)
    order = jnp.arange(flat_ids.shape[0], dtype=jnp.int32)
    before = (order[None, :] < order[:, None]) & (flat_ids[None, :] == flat_ids[:, None])
    places = jnp.sum(before.astype(jnp.int32), axis=1)
    return (flat_ids * capacity + places).reshape(routes.shape)


def dispatch_rows(tokens, slot_ids, experts, capacity):
    numbered = jnp.arange(experts * capacity, dtype=jnp.int32)
    picker = jnp.any(slot_ids[None, :, :] == numbered[:, None, None], axis=2).astype(jnp.bfloat16)
    filled = jnp.dot(picker, tokens, preferred_element_type=jnp.float32).astype(jnp.bfloat16)
    return jnp.repeat(filled.reshape(experts, capacity, tokens.shape[1]), HSPLIT, axis=0)


def combine_rows(base, returned, slot_ids, weights, experts, capacity):
    width = base.shape[1]
    summed = jnp.sum(returned.astype(jnp.float32).reshape(experts, HSPLIT, capacity, width), axis=1)
    summed = summed.reshape(experts * capacity, width)
    numbered = jnp.arange(experts * capacity, dtype=jnp.int32)
    mixing = jnp.sum(
        weights[:, :, None] * (slot_ids[:, :, None] == numbered[None, None, :]).astype(jnp.float32),
        axis=1,
    )
    total = base.astype(jnp.float32) + jnp.dot(mixing, summed, precision=lax.Precision.HIGHEST)
    return total.astype(jnp.bfloat16)


def forward_rows(received, gate_cols, up_cols, down_rows):
    in_shape = received.shape
    row_block = received.reshape(-1, in_shape[-1])
    pre_gate = jnp.dot(row_block, gate_cols, preferred_element_type=jnp.float32)
    pre_up = jnp.dot(row_block, up_cols, preferred_element_type=jnp.float32)
    hidden = (jax.nn.silu(pre_gate) * pre_up).astype(jnp.bfloat16)
    result = jnp.dot(hidden, down_rows, preferred_element_type=jnp.float32).astype(jnp.bfloat16)
    return result.reshape(in_shape)


def backward_rows(received_x, received_g, gate_cols, up_cols, down_rows):
    in_shape = received_x.shape
    rows_x = received_x.reshape(-1, in_shape[-1])
    rows_g = received_g.reshape(-1, in_shape[-1])
    contract = (((1,), (1,)), ((), ()))
    pre_gate = jnp.dot(rows_x, gate_cols, preferred_element_type=jnp.float32)
    pre_up = jnp.dot(rows_x, up_cols, preferred_element_type=jnp.float32)
    act_grad = lax.dot_general(rows_g, down_rows, contract, preferred_element_type=jnp.float32)
    sigmoid_gate = jax.nn.sigmoid(pre_gate)
    gate_grad = (act_grad * pre_up * sigmoid_gate * (1.0 + pre_gate * (1.0 - sigmoid_gate))).astype(
        jnp.bfloat16
    )
    up_grad = (act_grad * pre_gate * sigmoid_gate).astype(jnp.bfloat16)
    back_rows = lax.dot_general(gate_grad, gate_cols, contract, preferred_element_type=jnp.float32)
    back_rows = back_rows + lax.dot_general(
        up_grad, up_cols, contract, preferred_element_type=jnp.float32
    )
    return back_rows.astype(jnp.bfloat16).reshape(in_shape)


def body(
    x_fwd,
    routes_fwd,
    gates_fwd,
    x_bwd,
    grad_bwd,
    routes_bwd,
    gates_bwd,
    gate_proj,
    up_proj,
    down_proj,
):
    tokens_a = x_fwd[0]
    tokens_b = x_bwd[0]
    grads_b = grad_bwd[0]
    gate_cols = gate_proj[0]
    up_cols = up_proj[0]
    down_rows = down_proj[0]
    experts = lax.axis_size("expert") // HSPLIT
    tok_rows = tokens_a.shape[0]
    capacity = min(tok_rows, tok_rows * TOPK * 3 // (2 * experts))
    slots_a = slot_table(routes_fwd[0], experts, capacity)
    slots_b = slot_table(routes_bwd[0], experts, capacity)
    send_a = dispatch_rows(tokens_a, slots_a, experts, capacity)
    send_x = dispatch_rows(tokens_b, slots_b, experts, capacity)
    send_g = dispatch_rows(grads_b, slots_b, experts, capacity)
    back_a = lax.all_to_all(
        forward_rows(
            lax.all_to_all(send_a, "expert", split_axis=0, concat_axis=0, tiled=True),
            gate_cols,
            up_cols,
            down_rows,
        ),
        "expert",
        split_axis=0,
        concat_axis=0,
        tiled=True,
    )
    back_b = lax.all_to_all(
        backward_rows(
            lax.all_to_all(send_x, "expert", split_axis=0, concat_axis=0, tiled=True),
            lax.all_to_all(send_g, "expert", split_axis=0, concat_axis=0, tiled=True),
            gate_cols,
            up_cols,
            down_rows,
        ),
        "expert",
        split_axis=0,
        concat_axis=0,
        tiled=True,
    )
    out_fwd = combine_rows(tokens_a, back_a, slots_a, gates_fwd[0], experts, capacity)
    out_bwd = combine_rows(grads_b, back_b, slots_b, gates_bwd[0], experts, capacity)
    fwd_next = shifted(out_fwd, "pipe", 1)
    bwd_next = shifted(out_bwd, "pipe", -1)
    return (fwd_next[None], bwd_next[None])


def solution(mesh):
    in_specs = (
        P("pipe", "expert", None),
        P("pipe", "expert", None),
        P("pipe", "expert", None),
        P("pipe", "expert", None),
        P("pipe", "expert", None),
        P("pipe", "expert", None),
        P("pipe", "expert", None),
        P("pipe", None, "expert"),
        P("pipe", None, "expert"),
        P("pipe", "expert", None),
    )
    out_specs = (P("pipe", "expert", None), P("pipe", "expert", None))
    return jax.shard_map(body, mesh=mesh, in_specs=in_specs, out_specs=out_specs, check_vma=False)
```

```python
import jax
import jax.numpy as jnp
from jax import lax
from jax.experimental import pallas as pl
from jax.experimental.pallas import tpu as pltpu
from jax.sharding import PartitionSpec as P

D = 3584
HALF = D // 2
HID = 256
TOK = 64
CAP = 12
MSG = 4 * CAP
ROWS = 8 * CAP
PAIRS = 4
STEPS = 4
BF = jnp.bfloat16
F32 = jnp.float32
NT = (((1,), (1,)), ((), ()))


def at(y, p, b, c):
    return ((y * PAIRS + p) * 2 + b) * 2 + c


def places_of():
    return [
        (y, p, b, c) for y in range(2) for p in range(PAIRS) for b in range(2) for c in range(2)
    ]


def near(step):
    pairs = []
    for y, p, b, c in places_of():
        if step == 0:
            dp, nb = 0, b
        elif step == 3:
            dp, nb = 2, 1 - b
        elif (step == 1) == (b == 0):
            dp, nb = 1, 0
        else:
            dp, nb = -1, 1
        pairs.append((at(y, p, b, c), at(c, (p + dp) % PAIRS, nb, y)))
    return pairs


def other_core(block):
    pairs = [(at(y, p, b, c), at(y, p, b, 1 - c)) for y, p, b, c in places_of()]
    return lax.ppermute(block, "expert", pairs)


def other_chip(block):
    pairs = [(at(y, p, b, c), at(y, p, 1 - b, c)) for y, p, b, c in places_of()]
    return lax.ppermute(block, "expert", pairs)


def to_section(block, distance, pairs):
    sections, members = lax.axis_size("pipe"), lax.axis_size("expert")
    route = [
        (s * members + i, (s + distance) * members + j)
        for s in range(sections)
        if 0 <= s + distance < sections
        for i, j in pairs
    ]
    return lax.ppermute(block, ("pipe", "expert"), route)


def vmem(n):
    return [pl.BlockSpec(memory_space=pltpu.VMEM)] * n


def call(kernel, outs, n_in, name, smem=0, flops=0, scratch=(), limit=40):
    return pl.pallas_call(
        kernel,
        out_shape=outs,
        in_specs=[pl.BlockSpec(memory_space=pltpu.SMEM)] * smem + vmem(n_in),
        out_specs=tuple(vmem(len(outs))),
        scratch_shapes=scratch,
        compiler_params=pltpu.CompilerParams(vmem_limit_bytes=limit * 2**20),
        cost_estimate=pl.CostEstimate(flops=flops, bytes_accessed=4_000_000, transcendentals=0),
        name=name,
    )


def row_numbers(me_ref, own_ref, other_ref, span):
    me = me_ref[0]
    core, chip, pair = me % 2, (me // 2) % 2, (me // 4) % PAIRS
    column = jnp.concatenate([own_ref[...], other_ref[...]], axis=0).astype(jnp.int32)
    n = 2 * TOK
    first = lax.broadcasted_iota(jnp.int32, (n, n), 0)
    second = lax.broadcasted_iota(jnp.int32, (n, n), 1)
    wide = jnp.broadcast_to(column, (n, n))
    line = jnp.sum(jnp.where(first == second, wide, 0), axis=0, keepdims=True)
    same_group = (first < TOK) == (second < TOK)
    before = (wide == line) & (first < second) & same_group
    place = jnp.sum(before.astype(jnp.int32), axis=0, keepdims=True)
    dp = ((line & 3) - pair + 4) & 3
    side = jnp.where(chip == 0, 1, 3)
    step = jnp.where(dp == 0, 0, jnp.where(dp == 2, 3, jnp.where(dp == side, 1, 2)))
    is_other = (lax.broadcasted_iota(jnp.int32, (1, n), 1) >= TOK).astype(jnp.int32)
    row = step * span + is_other * CAP + place
    return jnp.where((line >> 2) == core, row, -1)


def dispatch_kernel(me_ref, own_ids, other_ids, own_ref, other_ref, *outs):
    row = row_numbers(me_ref, own_ids, other_ids, 2 * CAP)
    pick = (lax.broadcasted_iota(jnp.int32, (ROWS, 2 * TOK), 0) == row).astype(BF)
    width = 256
    for j in range(HALF // width):
        parts = []
        for at_col in (j * width, HALF + j * width):
            columns = slice(at_col, at_col + width)
            tokens = jnp.concatenate([own_ref[:, columns], other_ref[:, columns]], axis=0)
            parts.append(jnp.dot(pick, tokens, preferred_element_type=F32))
        for s in range(STEPS):
            rows = slice(s * 2 * CAP, (s + 1) * 2 * CAP)
            block = jnp.concatenate([parts[0][rows], parts[1][rows]], axis=0)
            outs[s][:, j * width : (j + 1) * width] = block.astype(BF)


def join_kernel(*refs):
    out = refs[-1]
    for j in range(HALF // 256):
        columns = slice(j * 256, (j + 1) * 256)
        blocks = [r[:, columns].astype(F32) for r in refs[:-1]]
        low = jnp.concatenate([b[: 2 * CAP] for b in blocks], axis=0)
        high = jnp.concatenate([b[2 * CAP :] for b in blocks], axis=0)
        out[:, columns] = low.astype(BF)
        out[:, HALF + j * 256 : HALF + (j + 1) * 256] = high.astype(BF)


def stacked(refs):
    return jnp.concatenate([r[...] for r in refs], axis=0)


def forward_kernel(x0, x1, x2, x3, gate, up, down, o0, o1, o2, o3):
    rows = stacked((x0, x1, x2, x3))
    pre_gate = jnp.dot(rows, gate[...], preferred_element_type=F32)
    pre_up = jnp.dot(rows, up[...], preferred_element_type=F32)
    hidden = (jax.nn.silu(pre_gate) * pre_up).astype(BF)
    for j in range(D // 512):
        columns = slice(j * 512, (j + 1) * 512)
        part = jnp.dot(hidden, down[:, columns], preferred_element_type=F32).astype(BF)
        for k, o in enumerate((o0, o1, o2, o3)):
            o[:, columns] = part[k * ROWS : (k + 1) * ROWS]


def before_kernel(x0, x1, x2, x3, gate, up, pre_gate, pre_up):
    rows = stacked((x0, x1, x2, x3))
    pre_gate[...] = jnp.dot(rows, gate[...], preferred_element_type=F32)
    pre_up[...] = jnp.dot(rows, up[...], preferred_element_type=F32)


def backward_kernel(g0, g1, g2, g3, pre_gate_ref, pre_up_ref, gate, up, down, o0, o1, o2, o3):
    rows = stacked((g0, g1, g2, g3))
    act_grad = lax.dot_general(rows, down[...], NT, preferred_element_type=F32)
    pre_gate, pre_up = pre_gate_ref[...], pre_up_ref[...]
    sig = jax.nn.sigmoid(pre_gate)
    gate_grad = (act_grad * pre_up * sig * (1.0 + pre_gate * (1.0 - sig))).astype(BF)
    up_grad = (act_grad * pre_gate * sig).astype(BF)
    for j in range(D // 512):
        columns = slice(j * 512, (j + 1) * 512)
        part = lax.dot_general(gate_grad, gate[columns, :], NT, preferred_element_type=F32)
        part = part + lax.dot_general(up_grad, up[columns, :], NT, preferred_element_type=F32)
        part = part.astype(BF)
        for k, o in enumerate((o0, o1, o2, o3)):
            o[:, columns] = part[k * ROWS : (k + 1) * ROWS]


def add_kernel(a, b, o):
    o[...] = (a[...].astype(F32) + b[...].astype(F32)).astype(BF)


def split_kernel(a, b, c, *outs):
    for j in range(HALF // 256):
        parts = []
        for at_col in (j * 256, HALF + j * 256):
            columns = slice(at_col, at_col + 256)
            parts.append(
                a[:, columns].astype(F32) + b[:, columns].astype(F32) + c[:, columns].astype(F32)
            )
        for s in range(STEPS):
            rows = slice(s * 2 * CAP, (s + 1) * 2 * CAP)
            block = jnp.concatenate([parts[0][rows], parts[1][rows]], axis=0)
            outs[s][:, j * 256 : (j + 1) * 256] = block.astype(BF)


def pick_kernel(me_ref, own_ids, other_ids, m0, m1, m2, m3, mine, theirs):
    row = row_numbers(me_ref, own_ids, other_ids, MSG)
    where = lax.broadcasted_iota(jnp.int32, (STEPS * MSG, 2 * TOK), 0)
    low = (where == row).astype(F32).T.astype(BF)
    high = ((where == row + 2 * CAP) & (row >= 0)).astype(F32).T.astype(BF)
    for j in range(HALF // 256):
        columns = slice(j * 256, (j + 1) * 256)
        rows = jnp.concatenate([m[:, columns] for m in (m0, m1, m2, m3)], axis=0)
        for at_col, pick in ((j * 256, low), (HALF + j * 256, high)):
            got = jnp.dot(pick, rows, preferred_element_type=F32).astype(BF)
            mine[:, at_col : at_col + 256] = got[:TOK]
            theirs[:, at_col : at_col + 256] = got[TOK:]


def final_kernel(base, gates, mine, theirs, o):
    weight = gates[...]
    for j in range(D // 512):
        columns = slice(j * 512, (j + 1) * 512)
        row = mine[:, columns].astype(F32) + theirs[:, columns].astype(F32)
        o[:, columns] = (base[:, columns].astype(F32) + weight * row).astype(BF)


def shape(*dims, kind=BF):
    return jax.ShapeDtypeStruct(dims, kind)


def dispatch(me, own_ids, other_ids, own, other):
    outs = [shape(MSG, HALF)] * STEPS
    return call(dispatch_kernel, outs, 4, "dispatch", smem=1)(me, own_ids, other_ids, own, other)


def gather(messages):
    (own,) = call(join_kernel, [shape(ROWS, D)], STEPS, "join")(*messages)
    across = other_chip(own)
    beside = other_core(own)
    return own, beside, across, other_core(across)


def give_back(parts, distance):
    own, beside, across, diagonal = parts
    from_diagonal = other_core(diagonal)
    from_beside = other_core(beside)
    (chip_sum,) = call(add_kernel, [shape(ROWS, D)], 2, "chip_sum")(across, from_diagonal)
    from_across = other_chip(chip_sum)
    messages = call(split_kernel, [shape(MSG, HALF)] * STEPS, 3, "pair_sum")(
        own, from_beside, from_across
    )
    return [
        to_section(m, distance, [(j, i) for i, j in near(s)]) for s, m in enumerate(messages)
    ]


def finish(me, messages, base, meta):
    own_ids, other_ids, gates = meta[:, 0:1], meta[:, 1:2], meta[:, 2:3]
    mine, theirs = call(pick_kernel, [shape(TOK, D)] * 2, 6, "pick", smem=1)(
        me, own_ids, other_ids, *messages
    )
    (out,) = call(final_kernel, [shape(TOK, D)], 4, "final")(base, gates, mine, other_core(theirs))
    return out


def body(x_fwd, routes_fwd, gates_fwd, x_bwd, grad_bwd, routes_bwd, gates_bwd, gate, up, down):
    x_a, x_b, g_b = x_fwd[0], x_bwd[0], grad_bwd[0]
    gate, up, down = gate[0], up[0], down[0]
    me = lax.axis_index("expert").astype(jnp.int32).reshape(1)
    same = [(i, i) for i in range(lax.axis_size("expert"))]

    ids = jnp.concatenate([routes_fwd[0], routes_bwd[0]], axis=1)
    other_ids = other_core(ids)
    ids_a, ids_b = ids[:, 0:1], ids[:, 1:2]
    other_a, other_b = other_ids[:, 0:1], other_ids[:, 1:2]
    meta_a = jnp.concatenate([ids_a.astype(F32), other_a.astype(F32), gates_fwd[0]], axis=1)
    meta_b = jnp.concatenate([ids_b.astype(F32), other_b.astype(F32), gates_bwd[0]], axis=1)

    sent_a = dispatch(me, ids_a, other_a, x_a, other_core(x_a))
    sent_x = dispatch(me, ids_b, other_b, x_b, other_core(x_b))
    sent_g = dispatch(me, ids_b, other_b, g_b, other_core(g_b))
    got_a = [lax.ppermute(m, "expert", near(s)) for s, m in enumerate(sent_a)]
    got_x = [lax.ppermute(m, "expert", near(s)) for s, m in enumerate(sent_x)]
    got_g = [lax.ppermute(m, "expert", near(s)) for s, m in enumerate(sent_g)]

    base_a = to_section(x_a, 1, same)
    base_b = to_section(g_b, -1, same)
    meta_a = to_section(meta_a, 1, same)
    meta_b = to_section(meta_b, -1, same)

    rows_a = gather(got_a)
    rows_x = gather(got_x)
    rows_g = gather(got_g)

    outs = [shape(ROWS, D)] * 4
    parts_a = call(forward_kernel, outs, 7, "expert_fwd", flops=6 * 384 * D * HID)(
        *rows_a, gate, up, down
    )
    pre = call(
        before_kernel, [shape(384, HID, kind=F32)] * 2, 6, "expert_pre", flops=4 * 384 * D * HID
    )(*rows_x, gate, up)
    parts_b = call(backward_kernel, outs, 9, "expert_bwd", flops=6 * 384 * D * HID)(
        *rows_g, *pre, gate, up, down
    )
    back_a = give_back(parts_a, 1)
    back_b = give_back(parts_b, -1)
    fwd_next = finish(me, back_a, base_a, meta_a)
    bwd_next = finish(me, back_b, base_b, meta_b)
    return fwd_next[None], bwd_next[None]


def solution(mesh):
    rows, cols = P("pipe", "expert", None), P("pipe", None, "expert")
    in_specs = (rows,) * 7 + (cols, cols, rows)
    return jax.shard_map(
        body, mesh=mesh, in_specs=in_specs, out_specs=(rows, rows), check_vma=False
    )
```

```python
import jax
import jax.numpy as jnp
from jax import lax
from jax.experimental import pallas as pl
from jax.experimental.pallas import tpu as pltpu
from jax.sharding import PartitionSpec as P

D = 3584
HALF = D // 2
HID = 256
TOK = 64
CAP = 12
MSG = 4 * CAP
ROWS = 8 * CAP
PAIRS = 4
STEPS = 4
BF = jnp.bfloat16
F32 = jnp.float32
NT = (((1,), (1,)), ((), ()))


def at(y, p, b, c):
    return ((y * PAIRS + p) * 2 + b) * 2 + c


def places_of():
    return [
        (y, p, b, c) for y in range(2) for p in range(PAIRS) for b in range(2) for c in range(2)
    ]


def near(step):
    pairs = []
    for y, p, b, c in places_of():
        if step == 0:
            dp, nb = 2, 1 - b
        elif step == 3:
            dp, nb = 0, b
        elif (step == 1) == (b == 0):
            dp, nb = 1, 0
        else:
            dp, nb = -1, 1
        pairs.append((at(y, p, b, c), at(c, (p + dp) % PAIRS, nb, y)))
    return pairs


def other_core(block):
    pairs = [(at(y, p, b, c), at(y, p, b, 1 - c)) for y, p, b, c in places_of()]
    return lax.ppermute(block, "expert", pairs)


def other_chip(block):
    pairs = [(at(y, p, b, c), at(y, p, 1 - b, c)) for y, p, b, c in places_of()]
    return lax.ppermute(block, "expert", pairs)


def to_section(block, distance, pairs):
    sections, members = lax.axis_size("pipe"), lax.axis_size("expert")
    route = [
        (s * members + i, (s + distance) * members + j)
        for s in range(sections)
        if 0 <= s + distance < sections
        for i, j in pairs
    ]
    return lax.ppermute(block, ("pipe", "expert"), route)


def vmem(n):
    return [pl.BlockSpec(memory_space=pltpu.VMEM)] * n


def call(kernel, outs, n_in, name, smem=0, flops=0, scratch=(), limit=40):
    return pl.pallas_call(
        kernel,
        out_shape=outs,
        in_specs=[pl.BlockSpec(memory_space=pltpu.SMEM)] * smem + vmem(n_in),
        out_specs=tuple(vmem(len(outs))),
        scratch_shapes=scratch,
        compiler_params=pltpu.CompilerParams(vmem_limit_bytes=limit * 2**20),
        cost_estimate=pl.CostEstimate(flops=flops, bytes_accessed=0, transcendentals=0),
        name=name,
    )


def token_rows(me_ref, own_ref, other_ref):
    me = me_ref[0]
    core, chip, pair = me % 2, (me // 2) % 2, (me // 4) % PAIRS
    line = jnp.concatenate([own_ref[...], other_ref[...]], axis=1)
    n = 2 * TOK
    first = lax.broadcasted_iota(jnp.int32, (n, n), 0)
    second = lax.broadcasted_iota(jnp.int32, (n, n), 1)
    wide = jnp.broadcast_to(line, (n, n))
    column = jnp.sum(jnp.where(first == second, wide, 0), axis=1, keepdims=True)
    same_group = (first < TOK) == (second < TOK)
    before = (column == wide) & (first < second) & same_group
    place = jnp.sum(before.astype(jnp.int32), axis=0, keepdims=True)
    dp = ((line & 3) - pair + 4) & 3
    side = jnp.where(chip == 0, 1, 3)
    step = jnp.where(dp == 0, 3, jnp.where(dp == 2, 0, jnp.where(dp == side, 1, 2)))
    is_other = (lax.broadcasted_iota(jnp.int32, (1, n), 1) >= TOK).astype(jnp.int32)
    row = step * 2 * CAP + is_other * CAP + place
    return jnp.where((line >> 2) == core, row, -1)


def dispatch_kernel(me_ref, own_ids, other_ids, gates_ref, *refs):
    tokens, meta_ref, outs = refs[: -STEPS - 1], refs[-STEPS - 1], refs[-STEPS:]
    row = token_rows(me_ref, own_ids, other_ids)
    gates = jnp.concatenate([gates_ref[...], gates_ref[...]], axis=1)
    which = lax.broadcasted_iota(jnp.int32, (8, 2 * TOK), 0)
    meta_ref[...] = jnp.where(which == 0, row.astype(F32), jnp.where(which == 1, gates, 0.0))
    pick = (lax.broadcasted_iota(jnp.int32, (ROWS, 2 * TOK), 0) == row).astype(BF)
    width = 256
    for k in range(len(tokens) // 2):
        own_ref, other_ref = tokens[2 * k], tokens[2 * k + 1]
        for j in range(HALF // width):
            parts = []
            for at_col in (j * width, HALF + j * width):
                columns = slice(at_col, at_col + width)
                both = jnp.concatenate([own_ref[:, columns], other_ref[:, columns]], axis=0)
                parts.append(jnp.dot(pick, both, preferred_element_type=F32))
            for s in range(STEPS):
                rows = slice(s * 2 * CAP, (s + 1) * 2 * CAP)
                block = jnp.concatenate([parts[0][rows], parts[1][rows]], axis=0)
                outs[s][k * MSG : (k + 1) * MSG, j * width : (j + 1) * width] = block.astype(BF)


def join_kernel(*refs):
    out = refs[-1]
    for k in range(out.shape[0] // ROWS):
        at_row = slice(k * ROWS, (k + 1) * ROWS)
        for j in range(HALF // 256):
            columns = slice(j * 256, (j + 1) * 256)
            blocks = [r[k * MSG : (k + 1) * MSG, columns].astype(F32) for r in refs[:-1]]
            low = jnp.concatenate([b[: 2 * CAP] for b in blocks], axis=0)
            high = jnp.concatenate([b[2 * CAP :] for b in blocks], axis=0)
            out[at_row, columns] = low.astype(BF)
            out[at_row, HALF + j * 256 : HALF + (j + 1) * 256] = high.astype(BF)


def stacked(refs):
    return jnp.concatenate([r[...] for r in refs], axis=0)


def forward_kernel(x0, x1, x2, x3, gate, up, down, o0, o1, o2, o3):
    rows = stacked((x0, x1, x2, x3))
    pre_gate = jnp.dot(rows, gate[...], preferred_element_type=F32)
    pre_up = jnp.dot(rows, up[...], preferred_element_type=F32)
    hidden = (jax.nn.silu(pre_gate) * pre_up).astype(BF)
    for j in range(D // 512):
        columns = slice(j * 512, (j + 1) * 512)
        part = jnp.dot(hidden, down[:, columns], preferred_element_type=F32).astype(BF)
        for k, o in enumerate((o0, o1, o2, o3)):
            o[:, columns] = part[k * ROWS : (k + 1) * ROWS]


def backward_kernel(r0, r1, r2, r3, gate, up, down, o0, o1, o2, o3):
    rows_x = jnp.concatenate([r[:ROWS] for r in (r0, r1, r2, r3)], axis=0)
    pre_gate = jnp.dot(rows_x, gate[...], preferred_element_type=F32)
    pre_up = jnp.dot(rows_x, up[...], preferred_element_type=F32)
    rows_g = jnp.concatenate([r[ROWS:] for r in (r0, r1, r2, r3)], axis=0)
    act_grad = lax.dot_general(rows_g, down[...], NT, preferred_element_type=F32)
    sig = jax.nn.sigmoid(pre_gate)
    gate_grad = (act_grad * pre_up * sig * (1.0 + pre_gate * (1.0 - sig))).astype(BF)
    up_grad = (act_grad * pre_gate * sig).astype(BF)
    for j in range(D // 512):
        columns = slice(j * 512, (j + 1) * 512)
        part = lax.dot_general(gate_grad, gate[columns, :], NT, preferred_element_type=F32)
        part = part + lax.dot_general(up_grad, up[columns, :], NT, preferred_element_type=F32)
        part = part.astype(BF)
        for k, o in enumerate((o0, o1, o2, o3)):
            o[:, columns] = part[k * ROWS : (k + 1) * ROWS]


def add_kernel(a, b, o):
    o[...] = (a[...].astype(F32) + b[...].astype(F32)).astype(BF)


def split_kernel(a, b, c, *outs):
    for j in range(HALF // 256):
        parts = []
        for at_col in (j * 256, HALF + j * 256):
            columns = slice(at_col, at_col + 256)
            parts.append(
                a[:, columns].astype(F32) + b[:, columns].astype(F32) + c[:, columns].astype(F32)
            )
        for s in range(STEPS):
            rows = slice(s * 2 * CAP, (s + 1) * 2 * CAP)
            block = jnp.concatenate([parts[0][rows], parts[1][rows]], axis=0)
            outs[s][:, j * 256 : (j + 1) * 256] = block.astype(BF)


def pick_kernel(meta_ref, m0, m1, m2, m3, mine, theirs):
    row = meta_ref[0:1, :].astype(jnp.int32)
    step = jnp.where(row < 2 * CAP, 0, jnp.where(row < 4 * CAP, 1, jnp.where(row < 6 * CAP, 2, 3)))
    row = jnp.where(row < 0, -MSG, row + step * 2 * CAP)
    where = lax.broadcasted_iota(jnp.int32, (STEPS * MSG, 2 * TOK), 0)
    low = (where == row).astype(F32).T.astype(BF)
    high = (where == row + 2 * CAP).astype(F32).T.astype(BF)
    for j in range(HALF // 256):
        columns = slice(j * 256, (j + 1) * 256)
        rows = jnp.concatenate([m[:, columns] for m in (m0, m1, m2, m3)], axis=0)
        for at_col, pick in ((j * 256, low), (HALF + j * 256, high)):
            got = jnp.dot(pick, rows, preferred_element_type=F32).astype(BF)
            mine[:, at_col : at_col + 256] = got[:TOK]
            theirs[:, at_col : at_col + 256] = got[TOK:]


def final_kernel(meta_ref, base, mine, theirs, o):
    n = 2 * TOK
    diagonal = lax.broadcasted_iota(jnp.int32, (TOK, n), 0) == lax.broadcasted_iota(
        jnp.int32, (TOK, n), 1
    )
    gates = jnp.broadcast_to(meta_ref[1:2, :], (TOK, n))
    weight = jnp.sum(jnp.where(diagonal, gates, 0.0), axis=1, keepdims=True)
    for j in range(D // 512):
        columns = slice(j * 512, (j + 1) * 512)
        row = mine[:, columns].astype(F32) + theirs[:, columns].astype(F32)
        o[:, columns] = (base[:, columns].astype(F32) + weight * row).astype(BF)


def shape(*dims, kind=BF):
    return jax.ShapeDtypeStruct(dims, kind)


def after(value, *earlier):
    return lax.optimization_barrier((value, earlier))[0]


def dispatch(me, own_ids, other_ids, gates, *tokens):
    outs = [shape(8, 2 * TOK, kind=F32)] + [shape(MSG * (len(tokens) // 2), HALF)] * STEPS
    meta, *messages = call(dispatch_kernel, outs, 3 + len(tokens), "dispatch", smem=1)(
        me, own_ids, other_ids, gates, *tokens
    )
    return meta, messages


def send(messages, distance=0):
    if distance:
        return [to_section(m, distance, [(j, i) for i, j in near(s)]) for s, m in enumerate(messages)]
    return [lax.ppermute(m, "expert", near(s)) for s, m in enumerate(messages)]


def join(messages):
    rows = messages[0].shape[0] * 2
    (own,) = call(join_kernel, [shape(rows, D)], STEPS, "join")(*messages)
    return own


def core_sums(parts, *earlier):
    own, beside, across, diagonal = parts
    diagonal = after(diagonal, *earlier)
    from_diagonal = other_core(diagonal)
    from_beside = other_core(beside)
    (chip_sum,) = call(add_kernel, [shape(ROWS, D)], 2, "chip_sum")(across, from_diagonal)
    return own, from_beside, chip_sum


def pair_sums(own, from_beside, from_across):
    return call(split_kernel, [shape(MSG, HALF)] * STEPS, 3, "pair_sum")(
        own, from_beside, from_across
    )


def finish(messages, base, meta):
    mine, theirs = call(pick_kernel, [shape(TOK, D)] * 2, 5, "pick")(meta, *messages)
    (out,) = call(final_kernel, [shape(TOK, D)], 4, "final")(meta, base, mine, other_core(theirs))
    return out


def body(x_fwd, routes_fwd, gates_fwd, x_bwd, grad_bwd, routes_bwd, gates_bwd, gate, up, down):
    x_a, x_b, g_b = x_fwd[0], x_bwd[0], grad_bwd[0]
    gate, up, down = gate[0], up[0], down[0]
    me = lax.axis_index("expert").astype(jnp.int32).reshape(1)
    same = [(i, i) for i in range(lax.axis_size("expert"))]
    ids_a, ids_b = routes_fwd.reshape(1, TOK), routes_bwd.reshape(1, TOK)
    gates_a, gates_b = gates_fwd.reshape(1, TOK), gates_bwd.reshape(1, TOK)

    other_a, x_a_other = other_core(ids_a), other_core(x_a)
    others_b = other_core(ids_b), other_core(x_b), other_core(g_b)
    meta_a, sent_a = dispatch(me, ids_a, other_a, gates_a, x_a, x_a_other)
    meta_b, sent_b = dispatch(me, ids_b, others_b[0], gates_b, x_b, others_b[1], g_b, others_b[2])
    got_a = send([*sent_a[:2], *after(sent_a[2:], meta_b)])
    got_b = send(after(sent_b, *got_a[1:]))

    own_a = join(got_a)
    across_a = other_chip(own_a)
    rows_a = (own_a, other_core(after(own_a, got_b[3])), across_a, other_core(across_a))
    own_b = join(got_b)
    across_b = other_chip(own_b)
    x_a, g_b, meta_a, meta_b = after((x_a, g_b, meta_a, meta_b), across_a, own_b)
    base_a = to_section(x_a, 1, same)
    base_b = to_section(g_b, -1, same)
    meta_a = to_section(meta_a, 1, same)
    meta_b = to_section(meta_b, -1, same)

    outs = [shape(ROWS, D)] * 4
    work = 6 * 384 * D * HID
    parts_a = call(forward_kernel, outs, 7, "expert_fwd", flops=work)(*rows_a, gate, up, down)
    own_a, beside_a, chip_a = core_sums(parts_a)
    across_b = after(across_b, chip_a, meta_a, meta_b, base_a, base_b)
    rows_b = (own_b, other_core(after(own_b, chip_a)), across_b, other_core(across_b))
    across_a = other_chip(after(chip_a, across_b))
    parts_b = call(backward_kernel, outs, 7, "expert_bwd", flops=2 * work)(*rows_b, gate, up, down)
    own_b, beside_b, chip_b = core_sums(parts_b, across_a)
    across_b = other_chip(after(chip_b, across_a))
    back_a = send(pair_sums(own_a, beside_a, across_a), 1)
    back_b = send(pair_sums(own_b, beside_b, across_b), -1)
    fwd_next = finish(back_a, base_a, meta_a)
    bwd_next = finish(back_b, base_b, meta_b)
    return fwd_next[None], bwd_next[None]


def solution(mesh):
    rows, cols = P("pipe", "expert", None), P("pipe", None, "expert")
    in_specs = (rows,) * 7 + (cols, cols, rows)
    return jax.shard_map(
        body, mesh=mesh, in_specs=in_specs, out_specs=(rows, rows), check_vma=False
    )
```

```python
import functools

import jax
import jax.numpy as jnp
from jax import lax
from jax.experimental import pallas as pl
from jax.experimental.pallas import tpu as pltpu
from jax.sharding import PartitionSpec as P

D = 3584
HALF = D // 2
HID = 256
TOK = 64
CAP = 12
MSG = 4 * CAP
ROWS = 8 * CAP
PAIRS = 4
STEPS = 4
BF = jnp.bfloat16
F32 = jnp.float32
NT = (((1,), (1,)), ((), ()))


def at(y, p, b, c):
    return ((y * PAIRS + p) * 2 + b) * 2 + c


def places_of():
    return [
        (y, p, b, c) for y in range(2) for p in range(PAIRS) for b in range(2) for c in range(2)
    ]


def near(step):
    pairs = []
    for y, p, b, c in places_of():
        if step == 0:
            dp, nb = 2, 1 - b
        elif step == 3:
            dp, nb = 0, b
        elif (step == 1) == (b == 0):
            dp, nb = 1, 0
        else:
            dp, nb = -1, 1
        pairs.append((at(y, p, b, c), at(c, (p + dp) % PAIRS, nb, y)))
    return pairs


def other_core(block):
    pairs = [(at(y, p, b, c), at(y, p, b, 1 - c)) for y, p, b, c in places_of()]
    return lax.ppermute(block, "expert", pairs)


def other_chip(block):
    pairs = [(at(y, p, b, c), at(y, p, 1 - b, c)) for y, p, b, c in places_of()]
    return lax.ppermute(block, "expert", pairs)


def to_section(block, distance, pairs):
    sections, members = lax.axis_size("pipe"), lax.axis_size("expert")
    route = [
        (s * members + i, (s + distance) % sections * members + j)
        for s in range(sections)
        for i, j in pairs
    ]
    return lax.ppermute(block, ("pipe", "expert"), route)


def vmem(n):
    return [pl.BlockSpec(memory_space=pltpu.VMEM)] * n


def call(kernel, outs, n_in, name, smem=0, flops=0, scratch=(), limit=40):
    scalars = [pl.BlockSpec(memory_space=pltpu.SMEM)] * smem
    return pl.pallas_call(
        kernel,
        out_shape=outs,
        in_specs=scalars + vmem(n_in),
        out_specs=tuple(vmem(len(outs))),
        scratch_shapes=scratch,
        compiler_params=pltpu.CompilerParams(vmem_limit_bytes=limit * 2**20),
        cost_estimate=pl.CostEstimate(flops=flops, bytes_accessed=0, transcendentals=0),
        name=name,
    )


def token_rows(me_ref, own_ref, other_ref):
    me = me_ref[0]
    core, chip, pair = me % 2, (me // 2) % 2, (me // 4) % PAIRS
    line = jnp.concatenate([own_ref[...], other_ref[...]], axis=1)
    n = 2 * TOK
    first = lax.broadcasted_iota(jnp.int32, (n, n), 0)
    second = lax.broadcasted_iota(jnp.int32, (n, n), 1)
    wide = jnp.broadcast_to(line, (n, n))
    column = jnp.sum(jnp.where(first == second, wide, 0), axis=1, keepdims=True)
    same_group = (first < TOK) == (second < TOK)
    before = (column == wide) & (first < second) & same_group
    place = jnp.sum(before.astype(jnp.int32), axis=0, keepdims=True)
    dp = ((line & 3) - pair + 4) & 3
    side = jnp.where(chip == 0, 1, 3)
    step = jnp.where(dp == 0, 3, jnp.where(dp == 2, 0, jnp.where(dp == side, 1, 2)))
    is_other = (lax.broadcasted_iota(jnp.int32, (1, n), 1) >= TOK).astype(jnp.int32)
    row = step * 2 * CAP + is_other * CAP + place
    return jnp.where((line >> 2) == core, row, -1)


def dispatch_kernel(me_ref, own_ids, other_ids, gates_ref, *refs):
    tokens, meta_ref, outs = refs[: -STEPS - 1], refs[-STEPS - 1], refs[-STEPS:]
    row = token_rows(me_ref, own_ids, other_ids)
    gates = jnp.concatenate([gates_ref[...], gates_ref[...]], axis=1)
    which = lax.broadcasted_iota(jnp.int32, (8, 2 * TOK), 0)
    meta_ref[...] = jnp.where(which == 0, row.astype(F32), jnp.where(which == 1, gates, 0.0))
    pick = (lax.broadcasted_iota(jnp.int32, (ROWS, 2 * TOK), 0) == row).astype(BF)
    width = 256
    for k in range(len(tokens) // 2):
        own_ref, other_ref = tokens[2 * k], tokens[2 * k + 1]
        for j in range(HALF // width):
            parts = []
            for at_col in (j * width, HALF + j * width):
                columns = slice(at_col, at_col + width)
                both = jnp.concatenate([own_ref[:, columns], other_ref[:, columns]], axis=0)
                parts.append(jnp.dot(pick, both, preferred_element_type=F32))
            for s in range(STEPS):
                rows = slice(s * 2 * CAP, (s + 1) * 2 * CAP)
                block = jnp.concatenate([parts[0][rows], parts[1][rows]], axis=0)
                outs[s][k * MSG : (k + 1) * MSG, j * width : (j + 1) * width] = block.astype(BF)


def join_kernel(*refs):
    messages, out = refs[:-1], refs[-1]
    size = 2 * CAP * len(messages)
    for k in range(out.shape[0] // size):
        at_row = slice(k * size, (k + 1) * size)
        for j in range(HALF // 256):
            columns = slice(j * 256, (j + 1) * 256)
            blocks = [r[k * MSG : (k + 1) * MSG, columns].astype(F32) for r in messages]
            low = jnp.concatenate([b[: 2 * CAP] for b in blocks], axis=0)
            high = jnp.concatenate([b[2 * CAP :] for b in blocks], axis=0)
            out[at_row, columns] = low.astype(BF)
            out[at_row, HALF + j * 256 : HALF + (j + 1) * 256] = high.astype(BF)


def stacked(refs, start=0):
    return jnp.concatenate([r[start : start + ROWS] for r in refs], axis=0)


def forward_kernel(*refs):
    gate, up, down, *outs = refs[4:]
    rows = stacked(refs[:4])
    pre_gate = jnp.dot(rows, gate[...], preferred_element_type=F32)
    pre_up = jnp.dot(rows, up[...], preferred_element_type=F32)
    hidden = (jax.nn.silu(pre_gate) * pre_up).astype(BF)
    for j in range(D // 512):
        columns = slice(j * 512, (j + 1) * 512)
        part = jnp.dot(hidden, down[:, columns], preferred_element_type=F32).astype(BF)
        start = 0
        for o in outs:
            o[:, columns] = part[start : start + o.shape[0]]
            start += o.shape[0]


def backward_kernel(*refs):
    gate, up, down, *outs = refs[4:]
    rows_x = stacked(refs[:4])
    pre_gate = jnp.dot(rows_x, gate[...], preferred_element_type=F32)
    pre_up = jnp.dot(rows_x, up[...], preferred_element_type=F32)
    rows_g = stacked(refs[:4], ROWS)
    act_grad = lax.dot_general(rows_g, down[...], NT, preferred_element_type=F32)
    sig = jax.nn.sigmoid(pre_gate)
    gate_grad = (act_grad * pre_up * sig * (1.0 + pre_gate * (1.0 - sig))).astype(BF)
    up_grad = (act_grad * pre_gate * sig).astype(BF)
    for j in range(D // 512):
        columns = slice(j * 512, (j + 1) * 512)
        part = lax.dot_general(gate_grad, gate[columns, :], NT, preferred_element_type=F32)
        part = part + lax.dot_general(up_grad, up[columns, :], NT, preferred_element_type=F32)
        part = part.astype(BF)
        start = 0
        for o in outs:
            o[:, columns] = part[start : start + o.shape[0]]
            start += o.shape[0]


def add_kernel(a, b, o):
    o[...] = (a[...].astype(F32) + b[...].astype(F32)).astype(BF)


def split_kernel(start, a, b, c, *outs):
    mine = slice(start, start + c.shape[0])
    for j in range(HALF // 256):
        parts = []
        for at_col in (j * 256, HALF + j * 256):
            columns = slice(at_col, at_col + 256)
            both = a[mine, columns].astype(F32) + b[mine, columns].astype(F32)
            parts.append(both + c[:, columns].astype(F32))
        for s, o in enumerate(outs):
            rows = slice(s * 2 * CAP, (s + 1) * 2 * CAP)
            block = jnp.concatenate([parts[0][rows], parts[1][rows]], axis=0)
            o[:, j * 256 : (j + 1) * 256] = block.astype(BF)


def pick_kernel(meta_ref, m0, m1, m2, m3, mine, theirs):
    row = meta_ref[0:1, :].astype(jnp.int32)
    step = jnp.where(row < 2 * CAP, 0, jnp.where(row < 4 * CAP, 1, jnp.where(row < 6 * CAP, 2, 3)))
    row = jnp.where(row < 0, -MSG, row + step * 2 * CAP)
    where = lax.broadcasted_iota(jnp.int32, (STEPS * MSG, 2 * TOK), 0)
    low = (where == row).astype(F32).T.astype(BF)
    high = (where == row + 2 * CAP).astype(F32).T.astype(BF)
    for j in range(HALF // 256):
        columns = slice(j * 256, (j + 1) * 256)
        rows = jnp.concatenate([m[:, columns] for m in (m0, m1, m2, m3)], axis=0)
        for at_col, pick in ((j * 256, low), (HALF + j * 256, high)):
            got = jnp.dot(pick, rows, preferred_element_type=F32).astype(BF)
            mine[:, at_col : at_col + 256] = got[:TOK]
            theirs[:, at_col : at_col + 256] = got[TOK:]


def final_kernel(keep_ref, meta_ref, base, mine, theirs, o):
    keep = keep_ref[0] != 0
    n = 2 * TOK
    diagonal = lax.broadcasted_iota(jnp.int32, (TOK, n), 0) == lax.broadcasted_iota(
        jnp.int32, (TOK, n), 1
    )
    gates = jnp.broadcast_to(meta_ref[1:2, :], (TOK, n))
    weight = jnp.sum(jnp.where(diagonal, gates, 0.0), axis=1, keepdims=True)
    for j in range(D // 512):
        columns = slice(j * 512, (j + 1) * 512)
        row = mine[:, columns].astype(F32) + theirs[:, columns].astype(F32)
        total = base[:, columns].astype(F32) + weight * row
        o[:, columns] = jnp.where(keep, total, 0.0).astype(BF)


def shape(*dims, kind=BF):
    return jax.ShapeDtypeStruct(dims, kind)


def after(value, *earlier):
    return lax.optimization_barrier((value, earlier))[0]


def dispatch(me, own_ids, other_ids, gates, *tokens):
    outs = [shape(8, 2 * TOK, kind=F32)] + [shape(MSG * (len(tokens) // 2), HALF)] * STEPS
    meta, *messages = call(dispatch_kernel, outs, 3 + len(tokens), "dispatch", smem=1)(
        me, own_ids, other_ids, gates, *tokens
    )
    return meta, messages


def send(messages, steps, distance=0):
    if distance:
        routes = [[(j, i) for i, j in near(s)] for s in steps]
        return [to_section(m, distance, route) for m, route in zip(messages, routes)]
    return [lax.ppermute(m, "expert", near(s)) for m, s in zip(messages, steps)]


def join(messages):
    rows = messages[0].shape[0] // MSG * 2 * CAP * len(messages)
    (own,) = call(join_kernel, [shape(rows, D)], len(messages), "join")(*messages)
    return own


def core_sums(parts):
    own, beside, *rest = parts
    n = len(rest) // 2
    from_diagonal = [other_core(piece) for piece in rest[n:]]
    from_beside = other_core(beside)
    sums = [
        call(add_kernel, [shape(*a.shape)], 2, "chip_sum")(a, b)[0]
        for a, b in zip(rest, from_diagonal)
    ]
    return own, from_beside, sums


def pair_sums(steps, own, from_beside, from_across):
    kernel = functools.partial(split_kernel, steps.start * 2 * CAP)
    outs = [shape(MSG, HALF)] * (steps.stop - steps.start)
    return call(kernel, outs, 3, "pair_sum")(own, from_beside, from_across)


def finish(keep, messages, base, meta):
    mine, theirs = call(pick_kernel, [shape(TOK, D)] * 2, 5, "pick")(meta, *messages)
    (out,) = call(final_kernel, [shape(TOK, D)], 4, "final", smem=1)(
        keep, meta, base, mine, other_core(theirs)
    )
    return out


def body(x_fwd, routes_fwd, gates_fwd, x_bwd, grad_bwd, routes_bwd, gates_bwd, gate, up, down):
    x_a, x_b, g_b = x_fwd[0], x_bwd[0], grad_bwd[0]
    gate, up, down = gate[0], up[0], down[0]
    me = lax.axis_index("expert").astype(jnp.int32).reshape(1)
    section = lax.axis_index("pipe").astype(jnp.int32).reshape(1)
    last = lax.axis_size("pipe") - 1
    keep_a, keep_b = (section != 0).astype(jnp.int32), (section != last).astype(jnp.int32)
    same = [(i, i) for i in range(lax.axis_size("expert"))]
    ids_a, ids_b = routes_fwd.reshape(1, TOK), routes_bwd.reshape(1, TOK)
    gates_a, gates_b = gates_fwd.reshape(1, TOK), gates_bwd.reshape(1, TOK)

    other_a, x_a_other = other_core(ids_a), other_core(x_a)
    others_b = other_core(ids_b), other_core(x_b), other_core(g_b)
    meta_a, sent_a = dispatch(me, ids_a, other_a, gates_a, x_a, x_a_other)
    meta_b, sent_b = dispatch(me, ids_b, others_b[0], gates_b, x_b, others_b[1], g_b, others_b[2])
    got_a = send([*sent_a[:2], *after(sent_a[2:], meta_b)], range(STEPS))
    got_b = send(after(sent_b, *got_a[1:]), range(STEPS))

    own_a = join(got_a)
    across_a = other_chip(own_a)
    rows_a = (own_a, other_core(after(own_a, got_b[3])), across_a, other_core(across_a))
    own_b = join(got_b)
    across_b = other_chip(own_b)
    x_a, g_b, meta_a, meta_b = after((x_a, g_b, meta_a, meta_b), across_a, own_b)
    base_a = to_section(x_a, 1, same)
    base_b = to_section(g_b, -1, same)
    meta_a = to_section(meta_a, 1, same)
    meta_b = to_section(meta_b, -1, same)

    outs = [shape(ROWS, D)] * 4
    work = 6 * 384 * D * HID
    parts_a = call(forward_kernel, outs, 7, "expert_fwd", flops=work)(*rows_a, gate, up, down)
    own_a, beside_a, chip_a = core_sums(parts_a)
    across_b = after(across_b, *chip_a, meta_a, meta_b, base_a, base_b)
    rows_b = (own_b, other_core(after(own_b, *chip_a)), across_b, other_core(across_b))
    back_a = other_chip(after(chip_a[0], across_b))
    outs = outs[:2] + [shape(ROWS // 2, D)] * 4
    parts_b = call(backward_kernel, outs, 7, "expert_bwd", flops=2 * work)(*rows_b, gate, up, down)
    own_b, beside_b, chip_b = core_sums(parts_b)
    back_b0 = other_chip(chip_b[0])
    sums_a = pair_sums(slice(0, STEPS), after(own_a, *chip_b), beside_a, back_a)
    back_b1 = other_chip(after(chip_b[1], back_b0, sums_a[0]))
    got_a = send(sums_a[:1], (0,), 1)
    got_a += send(after(sums_a[1:], back_b0, got_a[0]), (1, 2, 3), 1)
    got_b = send(pair_sums(slice(0, 2), own_b, beside_b, back_b0), (0, 1), -1)
    got_b += send(pair_sums(slice(2, 4), own_b, beside_b, back_b1), (2, 3), -1)
    fwd_next = finish(keep_a, got_a, base_a, meta_a)
    bwd_next = finish(keep_b, got_b, base_b, meta_b)
    return fwd_next[None], bwd_next[None]


def solution(mesh):
    rows, cols = P("pipe", "expert", None), P("pipe", None, "expert")
    in_specs = (rows,) * 7 + (cols, cols, rows)
    return jax.shard_map(
        body, mesh=mesh, in_specs=in_specs, out_specs=(rows, rows), check_vma=False
    )
```

```python
import functools

import jax
import jax.numpy as jnp
from jax import lax
from jax.experimental import pallas as pl
from jax.experimental.pallas import tpu as pltpu
from jax.sharding import PartitionSpec as P

D = 3584
HALF = D // 2
HID = 256
TOK = 64
CAP = 12
MSG = 4 * CAP
ROWS = 8 * CAP
PAIRS = 4
STEPS = 4
BF = jnp.bfloat16
F32 = jnp.float32
NT = (((1,), (1,)), ((), ()))


def at(y, p, b, c):
    return ((y * PAIRS + p) * 2 + b) * 2 + c


def places_of():
    return [
        (y, p, b, c) for y in range(2) for p in range(PAIRS) for b in range(2) for c in range(2)
    ]


def near(step):
    pairs = []
    for y, p, b, c in places_of():
        if step == 0:
            dp, nb = 2, 1 - b
        elif step == 3:
            dp, nb = 0, b
        elif (step == 1) == (b == 0):
            dp, nb = 1, 0
        else:
            dp, nb = -1, 1
        pairs.append((at(y, p, b, c), at(c, (p + dp) % PAIRS, nb, y)))
    return pairs


def other_core(block):
    pairs = [(at(y, p, b, c), at(y, p, b, 1 - c)) for y, p, b, c in places_of()]
    return lax.ppermute(block, "expert", pairs)


def other_chip(block):
    pairs = [(at(y, p, b, c), at(y, p, 1 - b, c)) for y, p, b, c in places_of()]
    return lax.ppermute(block, "expert", pairs)


def to_section(block, distance, pairs):
    sections, members = lax.axis_size("pipe"), lax.axis_size("expert")
    route = [
        (s * members + i, (s + distance) % sections * members + j)
        for s in range(sections)
        for i, j in pairs
    ]
    return lax.ppermute(block, ("pipe", "expert"), route)


def vmem(n):
    return [pl.BlockSpec(memory_space=pltpu.VMEM)] * n


def call(kernel, outs, n_in, name, smem=0, flops=0, scratch=(), limit=40):
    scalars = [pl.BlockSpec(memory_space=pltpu.SMEM)] * smem
    return pl.pallas_call(
        kernel,
        out_shape=outs,
        in_specs=scalars + vmem(n_in),
        out_specs=tuple(vmem(len(outs))),
        scratch_shapes=scratch,
        compiler_params=pltpu.CompilerParams(vmem_limit_bytes=limit * 2**20),
        cost_estimate=pl.CostEstimate(flops=flops, bytes_accessed=0, transcendentals=0),
        name=name,
    )


def token_rows(me_ref, own_ref, other_ref):
    me = me_ref[0]
    core, chip, pair = me % 2, (me // 2) % 2, (me // 4) % PAIRS
    line = jnp.concatenate([own_ref[...], other_ref[...]], axis=1)
    n = 2 * TOK
    first = lax.broadcasted_iota(jnp.int32, (n, n), 0)
    second = lax.broadcasted_iota(jnp.int32, (n, n), 1)
    wide = jnp.broadcast_to(line, (n, n))
    column = jnp.sum(jnp.where(first == second, wide, 0), axis=1, keepdims=True)
    same_group = (first < TOK) == (second < TOK)
    before = (column == wide) & (first < second) & same_group
    place = jnp.sum(before.astype(jnp.int32), axis=0, keepdims=True)
    dp = ((line & 3) - pair + 4) & 3
    side = jnp.where(chip == 0, 1, 3)
    step = jnp.where(dp == 0, 3, jnp.where(dp == 2, 0, jnp.where(dp == side, 1, 2)))
    is_other = (lax.broadcasted_iota(jnp.int32, (1, n), 1) >= TOK).astype(jnp.int32)
    row = step * 2 * CAP + is_other * CAP + place
    return jnp.where((line >> 2) == core, row, -1)


def dispatch_kernel(me_ref, own_ids, other_ids, gates_ref, *refs):
    tokens, meta_ref, outs = refs[: -STEPS - 1], refs[-STEPS - 1], refs[-STEPS:]
    row = token_rows(me_ref, own_ids, other_ids)
    gates = jnp.concatenate([gates_ref[...], gates_ref[...]], axis=1)
    which = lax.broadcasted_iota(jnp.int32, (8, 2 * TOK), 0)
    meta_ref[...] = jnp.where(which == 0, row.astype(F32), jnp.where(which == 1, gates, 0.0))
    pick = (lax.broadcasted_iota(jnp.int32, (ROWS, 2 * TOK), 0) == row).astype(BF)
    width = 256
    for k in range(len(tokens) // 2):
        own_ref, other_ref = tokens[2 * k], tokens[2 * k + 1]
        for j in range(HALF // width):
            parts = []
            for at_col in (j * width, HALF + j * width):
                columns = slice(at_col, at_col + width)
                both = jnp.concatenate([own_ref[:, columns], other_ref[:, columns]], axis=0)
                parts.append(jnp.dot(pick, both, preferred_element_type=F32))
            for s in range(STEPS):
                rows = slice(s * 2 * CAP, (s + 1) * 2 * CAP)
                block = jnp.concatenate([parts[0][rows], parts[1][rows]], axis=0)
                outs[s][k * MSG : (k + 1) * MSG, j * width : (j + 1) * width] = block.astype(BF)


def join_kernel(*refs):
    messages, out = refs[:-1], refs[-1]
    size = 2 * CAP * len(messages)
    for k in range(out.shape[0] // size):
        at_row = slice(k * size, (k + 1) * size)
        for j in range(HALF // 256):
            columns = slice(j * 256, (j + 1) * 256)
            blocks = [r[k * MSG : (k + 1) * MSG, columns].astype(F32) for r in messages]
            low = jnp.concatenate([b[: 2 * CAP] for b in blocks], axis=0)
            high = jnp.concatenate([b[2 * CAP :] for b in blocks], axis=0)
            out[at_row, columns] = low.astype(BF)
            out[at_row, HALF + j * 256 : HALF + (j + 1) * 256] = high.astype(BF)


def stacked(refs, start=0):
    return jnp.concatenate([r[start : start + ROWS] for r in refs], axis=0)


def forward_kernel(*refs):
    gate, up, down, *outs = refs[4:]
    rows = stacked(refs[:4])
    pre_gate = jnp.dot(rows, gate[...], preferred_element_type=F32)
    pre_up = jnp.dot(rows, up[...], preferred_element_type=F32)
    hidden = (jax.nn.silu(pre_gate) * pre_up).astype(BF)
    for j in range(D // 512):
        columns = slice(j * 512, (j + 1) * 512)
        part = jnp.dot(hidden, down[:, columns], preferred_element_type=F32).astype(BF)
        start = 0
        for o in outs:
            o[:, columns] = part[start : start + o.shape[0]]
            start += o.shape[0]


def backward_kernel(*refs):
    gate, up, down, *outs = refs[4:]
    rows_x = stacked(refs[:4])
    pre_gate = jnp.dot(rows_x, gate[...], preferred_element_type=F32)
    pre_up = jnp.dot(rows_x, up[...], preferred_element_type=F32)
    rows_g = stacked(refs[:4], ROWS)
    act_grad = lax.dot_general(rows_g, down[...], NT, preferred_element_type=F32)
    sig = jax.nn.sigmoid(pre_gate)
    gate_grad = (act_grad * pre_up * sig * (1.0 + pre_gate * (1.0 - sig))).astype(BF)
    up_grad = (act_grad * pre_gate * sig).astype(BF)
    for j in range(D // 512):
        columns = slice(j * 512, (j + 1) * 512)
        part = lax.dot_general(gate_grad, gate[columns, :], NT, preferred_element_type=F32)
        part = part + lax.dot_general(up_grad, up[columns, :], NT, preferred_element_type=F32)
        part = part.astype(BF)
        start = 0
        for o in outs:
            o[:, columns] = part[start : start + o.shape[0]]
            start += o.shape[0]


def add_kernel(a, b, o):
    o[...] = (a[...].astype(F32) + b[...].astype(F32)).astype(BF)


def split_kernel(start, a, b, c, *outs):
    mine = slice(start, start + c.shape[0])
    for j in range(HALF // 256):
        parts = []
        for at_col in (j * 256, HALF + j * 256):
            columns = slice(at_col, at_col + 256)
            both = a[mine, columns].astype(F32) + b[mine, columns].astype(F32)
            parts.append(both + c[:, columns].astype(F32))
        for s, o in enumerate(outs):
            rows = slice(s * 2 * CAP, (s + 1) * 2 * CAP)
            block = jnp.concatenate([parts[0][rows], parts[1][rows]], axis=0)
            o[:, j * 256 : (j + 1) * 256] = block.astype(BF)


def pick_kernel(meta_ref, m0, m1, m2, m3, mine, theirs):
    row = meta_ref[0:1, :].astype(jnp.int32)
    step = jnp.where(row < 2 * CAP, 0, jnp.where(row < 4 * CAP, 1, jnp.where(row < 6 * CAP, 2, 3)))
    row = jnp.where(row < 0, -MSG, row + step * 2 * CAP)
    where = lax.broadcasted_iota(jnp.int32, (STEPS * MSG, 2 * TOK), 0)
    low = (where == row).astype(F32).T.astype(BF)
    high = (where == row + 2 * CAP).astype(F32).T.astype(BF)
    for j in range(HALF // 256):
        columns = slice(j * 256, (j + 1) * 256)
        rows = jnp.concatenate([m[:, columns] for m in (m0, m1, m2, m3)], axis=0)
        for at_col, pick in ((j * 256, low), (HALF + j * 256, high)):
            got = jnp.dot(pick, rows, preferred_element_type=F32).astype(BF)
            mine[:, at_col : at_col + 256] = got[:TOK]
            theirs[:, at_col : at_col + 256] = got[TOK:]


def final_kernel(keep_ref, meta_ref, base, mine, theirs, o):
    keep = keep_ref[0] != 0
    n = 2 * TOK
    diagonal = lax.broadcasted_iota(jnp.int32, (TOK, n), 0) == lax.broadcasted_iota(
        jnp.int32, (TOK, n), 1
    )
    gates = jnp.broadcast_to(meta_ref[1:2, :], (TOK, n))
    weight = jnp.sum(jnp.where(diagonal, gates, 0.0), axis=1, keepdims=True)
    for j in range(D // 512):
        columns = slice(j * 512, (j + 1) * 512)
        row = mine[:, columns].astype(F32) + theirs[:, columns].astype(F32)
        total = base[:, columns].astype(F32) + weight * row
        o[:, columns] = jnp.where(keep, total, 0.0).astype(BF)


def shape(*dims, kind=BF):
    return jax.ShapeDtypeStruct(dims, kind)


def after(value, *earlier):
    return lax.optimization_barrier((value, earlier))[0]


def dispatch(me, own_ids, other_ids, gates, *tokens):
    outs = [shape(8, 2 * TOK, kind=F32)] + [shape(MSG * (len(tokens) // 2), HALF)] * STEPS
    meta, *messages = call(dispatch_kernel, outs, 3 + len(tokens), "dispatch", smem=1)(
        me, own_ids, other_ids, gates, *tokens
    )
    return meta, messages


def send(messages, steps, distance=0):
    if distance:
        routes = [[(j, i) for i, j in near(s)] for s in steps]
        return [to_section(m, distance, route) for m, route in zip(messages, routes)]
    return [lax.ppermute(m, "expert", near(s)) for m, s in zip(messages, steps)]


def join(messages):
    rows = messages[0].shape[0] // MSG * 2 * CAP * len(messages)
    (own,) = call(join_kernel, [shape(rows, D)], len(messages), "join")(*messages)
    return own


def core_sums(parts):
    own, beside, *rest = parts
    n = len(rest) // 2
    from_diagonal = [other_core(piece) for piece in rest[n:]]
    from_beside = other_core(beside)
    sums = [
        call(add_kernel, [shape(*a.shape)], 2, "chip_sum")(a, b)[0]
        for a, b in zip(rest, from_diagonal)
    ]
    return own, from_beside, sums


def pair_sums(steps, own, from_beside, from_across):
    kernel = functools.partial(split_kernel, steps.start * 2 * CAP)
    outs = [shape(MSG, HALF)] * (steps.stop - steps.start)
    return call(kernel, outs, 3, "pair_sum")(own, from_beside, from_across)


def finish(keep, messages, base, meta):
    mine, theirs = call(pick_kernel, [shape(TOK, D)] * 2, 5, "pick")(meta, *messages)
    (out,) = call(final_kernel, [shape(TOK, D)], 4, "final", smem=1)(
        keep, meta, base, mine, other_core(theirs)
    )
    return out


def body(x_fwd, routes_fwd, gates_fwd, x_bwd, grad_bwd, routes_bwd, gates_bwd, gate, up, down):
    x_a, x_b, g_b = x_fwd[0], x_bwd[0], grad_bwd[0]
    gate, up, down = gate[0], up[0], down[0]
    me = lax.axis_index("expert").astype(jnp.int32).reshape(1)
    section = lax.axis_index("pipe").astype(jnp.int32).reshape(1)
    last = lax.axis_size("pipe") - 1
    keep_a, keep_b = (section != 0).astype(jnp.int32), (section != last).astype(jnp.int32)
    same = [(i, i) for i in range(lax.axis_size("expert"))]
    ids_a, ids_b = routes_fwd.reshape(1, TOK), routes_bwd.reshape(1, TOK)
    gates_a, gates_b = gates_fwd.reshape(1, TOK), gates_bwd.reshape(1, TOK)

    other_a, x_a_other = other_core(ids_a), other_core(x_a)
    others_b = other_core(ids_b), other_core(x_b), other_core(g_b)
    me_a = after(me, *others_b)
    meta_a, sent_a = dispatch(me_a, ids_a, other_a, gates_a, x_a, x_a_other)
    got_a = send(sent_a, range(STEPS))
    late = after(ids_b, got_a[3])
    meta_b, sent_b = dispatch(me, late, others_b[0], gates_b, x_b, others_b[1], g_b, others_b[2])
    got_b = send(after(sent_b, *got_a[1:]), range(STEPS))

    own_a = join(after(got_a, meta_b))
    across_a = other_chip(own_a)
    rows_a = (own_a, other_core(after(own_a, got_b[3])), across_a, other_core(across_a))
    own_b = join(got_b)
    across_b = other_chip(own_b)
    x_a, g_b, meta_a, meta_b = after((x_a, g_b, meta_a, meta_b), across_a, own_b)
    base_a = to_section(x_a, 1, same)
    base_b = to_section(g_b, -1, same)
    meta_a = to_section(meta_a, 1, same)
    meta_b = to_section(meta_b, -1, same)

    outs = [shape(ROWS, D)] * 4
    work = 6 * 384 * D * HID
    parts_a = call(forward_kernel, outs, 7, "expert_fwd", flops=work)(*rows_a, gate, up, down)
    own_a, beside_a, chip_a = core_sums(parts_a)
    across_b = after(across_b, *chip_a, meta_a, meta_b, base_a, base_b)
    rows_b = (own_b, other_core(after(own_b, *chip_a)), across_b, other_core(across_b))
    back_a = other_chip(after(chip_a[0], across_b))
    outs = outs[:2] + [shape(ROWS // 2, D)] * 4
    parts_b = call(backward_kernel, outs, 7, "expert_bwd", flops=2 * work)(*rows_b, gate, up, down)
    own_b, beside_b, chip_b = core_sums(parts_b)
    back_b0 = other_chip(chip_b[0])
    sums_a = pair_sums(slice(0, STEPS), after(own_a, *chip_b), beside_a, back_a)
    back_b1 = other_chip(after(chip_b[1], back_b0, sums_a[0]))
    got_a = send(sums_a[:1], (0,), 1)
    got_a += send(after(sums_a[1:], back_b0, got_a[0]), (1, 2, 3), 1)
    got_b = send(pair_sums(slice(0, 2), own_b, beside_b, back_b0), (0, 1), -1)
    got_b += send(pair_sums(slice(2, 4), own_b, beside_b, back_b1), (2, 3), -1)
    fwd_next = finish(keep_a, got_a, base_a, meta_a)
    bwd_next = finish(keep_b, got_b, base_b, meta_b)
    return fwd_next[None], bwd_next[None]


def solution(mesh):
    rows, cols = P("pipe", "expert", None), P("pipe", None, "expert")
    in_specs = (rows,) * 7 + (cols, cols, rows)
    return jax.shard_map(
        body, mesh=mesh, in_specs=in_specs, out_specs=(rows, rows), check_vma=False
    )
```

```python
import functools

import jax
import jax.numpy as jnp
from jax import lax
from jax.experimental import pallas as pl
from jax.experimental.pallas import tpu as pltpu
from jax.sharding import PartitionSpec as P

D = 3584
HALF = D // 2
HID = 256
TOK = 64
CAP = 12
MSG = 4 * CAP
ROWS = 8 * CAP
PAIRS = 4
STEPS = 4
BF = jnp.bfloat16
F32 = jnp.float32
NT = (((1,), (1,)), ((), ()))


def at(y, p, b, c):
    return ((y * PAIRS + p) * 2 + b) * 2 + c


def places_of():
    return [
        (y, p, b, c) for y in range(2) for p in range(PAIRS) for b in range(2) for c in range(2)
    ]


def near(step):
    pairs = []
    for y, p, b, c in places_of():
        if step == 0:
            dp, nb = 2, 1 - b
        elif step == 3:
            dp, nb = 0, b
        elif (step == 1) == (b == 0):
            dp, nb = 1, 0
        else:
            dp, nb = -1, 1
        pairs.append((at(y, p, b, c), at(c, (p + dp) % PAIRS, nb, y)))
    return pairs


def other_core(block):
    pairs = [(at(y, p, b, c), at(y, p, b, 1 - c)) for y, p, b, c in places_of()]
    return lax.ppermute(block, "expert", pairs)


def other_chip(block):
    pairs = [(at(y, p, b, c), at(y, p, 1 - b, c)) for y, p, b, c in places_of()]
    return lax.ppermute(block, "expert", pairs)


def to_section(block, distance, pairs):
    sections, members = lax.axis_size("pipe"), lax.axis_size("expert")
    route = [
        (s * members + i, (s + distance) % sections * members + j)
        for s in range(sections)
        for i, j in pairs
    ]
    return lax.ppermute(block, ("pipe", "expert"), route)


def vmem(n):
    return [pl.BlockSpec(memory_space=pltpu.VMEM)] * n


def call(kernel, outs, n_in, name, smem=0, flops=0, scratch=(), limit=40):
    scalars = [pl.BlockSpec(memory_space=pltpu.SMEM)] * smem
    return pl.pallas_call(
        kernel,
        out_shape=outs,
        in_specs=scalars + vmem(n_in),
        out_specs=tuple(vmem(len(outs))),
        scratch_shapes=scratch,
        compiler_params=pltpu.CompilerParams(vmem_limit_bytes=limit * 2**20),
        cost_estimate=pl.CostEstimate(flops=flops, bytes_accessed=0, transcendentals=0),
        name=name,
    )


def token_rows(me_ref, own_ref, other_ref):
    me = me_ref[0]
    core, chip, pair = me % 2, (me // 2) % 2, (me // 4) % PAIRS
    line = jnp.concatenate([own_ref[...], other_ref[...]], axis=1)
    n = 2 * TOK
    first = lax.broadcasted_iota(jnp.int32, (n, n), 0)
    second = lax.broadcasted_iota(jnp.int32, (n, n), 1)
    wide = jnp.broadcast_to(line, (n, n))
    column = jnp.sum(jnp.where(first == second, wide, 0), axis=1, keepdims=True)
    same_group = (first < TOK) == (second < TOK)
    before = (column == wide) & (first < second) & same_group
    place = jnp.sum(before.astype(jnp.int32), axis=0, keepdims=True)
    dp = ((line & 3) - pair + 4) & 3
    side = jnp.where(chip == 0, 1, 3)
    step = jnp.where(dp == 0, 3, jnp.where(dp == 2, 0, jnp.where(dp == side, 1, 2)))
    is_other = (lax.broadcasted_iota(jnp.int32, (1, n), 1) >= TOK).astype(jnp.int32)
    row = step * 2 * CAP + is_other * CAP + place
    return jnp.where((line >> 2) == core, row, -1)


def dispatch_kernel(me_ref, own_ids, other_ids, *refs):
    tokens, meta_ref, outs = refs[: -STEPS - 1], refs[-STEPS - 1], refs[-STEPS:]
    row = token_rows(me_ref, own_ids, other_ids)
    meta_ref[...] = jnp.broadcast_to(row.astype(F32), meta_ref.shape)
    pick = (lax.broadcasted_iota(jnp.int32, (ROWS, 2 * TOK), 0) == row).astype(BF)
    width = 256
    for k in range(len(tokens) // 2):
        own_ref, other_ref = tokens[2 * k], tokens[2 * k + 1]
        for j in range(HALF // width):
            parts = []
            for at_col in (j * width, HALF + j * width):
                columns = slice(at_col, at_col + width)
                both = jnp.concatenate([own_ref[:, columns], other_ref[:, columns]], axis=0)
                parts.append(jnp.dot(pick, both, preferred_element_type=F32))
            for s in range(STEPS):
                rows = slice(s * 2 * CAP, (s + 1) * 2 * CAP)
                block = jnp.concatenate([parts[0][rows], parts[1][rows]], axis=0)
                outs[s][k * MSG : (k + 1) * MSG, j * width : (j + 1) * width] = block.astype(BF)


def meta_kernel(rows, gates_ref, o):
    gates = jnp.concatenate([gates_ref[...], gates_ref[...]], axis=1)
    which = lax.broadcasted_iota(jnp.int32, o.shape, 0)
    o[...] = jnp.where(which == 0, rows[...], gates)


def join_kernel(*refs):
    messages, out = refs[:-1], refs[-1]
    size = 2 * CAP * len(messages)
    for k in range(out.shape[0] // size):
        at_row = slice(k * size, (k + 1) * size)
        for j in range(HALF // 256):
            columns = slice(j * 256, (j + 1) * 256)
            blocks = [r[k * MSG : (k + 1) * MSG, columns].astype(F32) for r in messages]
            low = jnp.concatenate([b[: 2 * CAP] for b in blocks], axis=0)
            high = jnp.concatenate([b[2 * CAP :] for b in blocks], axis=0)
            out[at_row, columns] = low.astype(BF)
            out[at_row, HALF + j * 256 : HALF + (j + 1) * 256] = high.astype(BF)


def stacked(refs, start=0):
    return jnp.concatenate([r[start : start + ROWS] for r in refs], axis=0)


def forward_kernel(*refs):
    gate, up, down, *outs = refs[4:]
    rows = stacked(refs[:4])
    pre_gate = jnp.dot(rows, gate[...], preferred_element_type=F32)
    pre_up = jnp.dot(rows, up[...], preferred_element_type=F32)
    hidden = (jax.nn.silu(pre_gate) * pre_up).astype(BF)
    for j in range(D // 512):
        columns = slice(j * 512, (j + 1) * 512)
        part = jnp.dot(hidden, down[:, columns], preferred_element_type=F32).astype(BF)
        start = 0
        for o in outs:
            o[:, columns] = part[start : start + o.shape[0]]
            start += o.shape[0]


def backward_kernel(*refs):
    gate, up, down, *outs = refs[4:]
    rows_x = stacked(refs[:4])
    pre_gate = jnp.dot(rows_x, gate[...], preferred_element_type=F32)
    pre_up = jnp.dot(rows_x, up[...], preferred_element_type=F32)
    rows_g = stacked(refs[:4], ROWS)
    act_grad = lax.dot_general(rows_g, down[...], NT, preferred_element_type=F32)
    sig = jax.nn.sigmoid(pre_gate)
    gate_grad = (act_grad * pre_up * sig * (1.0 + pre_gate * (1.0 - sig))).astype(BF)
    up_grad = (act_grad * pre_gate * sig).astype(BF)
    for j in range(D // 512):
        columns = slice(j * 512, (j + 1) * 512)
        part = lax.dot_general(gate_grad, gate[columns, :], NT, preferred_element_type=F32)
        part = part + lax.dot_general(up_grad, up[columns, :], NT, preferred_element_type=F32)
        part = part.astype(BF)
        start = 0
        for o in outs:
            o[:, columns] = part[start : start + o.shape[0]]
            start += o.shape[0]


def add_kernel(a, b, o):
    o[...] = (a[...].astype(F32) + b[...].astype(F32)).astype(BF)


def split_kernel(start, a, b, c, *outs):
    mine = slice(start, start + c.shape[0])
    for j in range(HALF // 256):
        parts = []
        for at_col in (j * 256, HALF + j * 256):
            columns = slice(at_col, at_col + 256)
            both = a[mine, columns].astype(F32) + b[mine, columns].astype(F32)
            parts.append(both + c[:, columns].astype(F32))
        for s, o in enumerate(outs):
            rows = slice(s * 2 * CAP, (s + 1) * 2 * CAP)
            block = jnp.concatenate([parts[0][rows], parts[1][rows]], axis=0)
            o[:, j * 256 : (j + 1) * 256] = block.astype(BF)


def pick_kernel(meta_ref, m0, m1, m2, m3, mine, theirs):
    row = meta_ref[0:1, :].astype(jnp.int32)
    step = jnp.where(row < 2 * CAP, 0, jnp.where(row < 4 * CAP, 1, jnp.where(row < 6 * CAP, 2, 3)))
    row = jnp.where(row < 0, -MSG, row + step * 2 * CAP)
    where = lax.broadcasted_iota(jnp.int32, (STEPS * MSG, 2 * TOK), 0)
    low = (where == row).astype(F32).T.astype(BF)
    high = (where == row + 2 * CAP).astype(F32).T.astype(BF)
    for j in range(HALF // 256):
        columns = slice(j * 256, (j + 1) * 256)
        rows = jnp.concatenate([m[:, columns] for m in (m0, m1, m2, m3)], axis=0)
        for at_col, pick in ((j * 256, low), (HALF + j * 256, high)):
            got = jnp.dot(pick, rows, preferred_element_type=F32).astype(BF)
            mine[:, at_col : at_col + 256] = got[:TOK]
            theirs[:, at_col : at_col + 256] = got[TOK:]


def final_kernel(keep_ref, meta_ref, base, mine, theirs, o):
    keep = keep_ref[0] != 0
    n = 2 * TOK
    diagonal = lax.broadcasted_iota(jnp.int32, (TOK, n), 0) == lax.broadcasted_iota(
        jnp.int32, (TOK, n), 1
    )
    gates = jnp.broadcast_to(meta_ref[1:2, :], (TOK, n))
    weight = jnp.sum(jnp.where(diagonal, gates, 0.0), axis=1, keepdims=True)
    for j in range(D // 512):
        columns = slice(j * 512, (j + 1) * 512)
        row = mine[:, columns].astype(F32) + theirs[:, columns].astype(F32)
        total = base[:, columns].astype(F32) + weight * row
        o[:, columns] = jnp.where(keep, total, 0.0).astype(BF)


def shape(*dims, kind=BF):
    return jax.ShapeDtypeStruct(dims, kind)


def after(value, *earlier):
    return lax.optimization_barrier((value, earlier))[0]


def with_gates(rows, gates):
    (meta,) = call(meta_kernel, [shape(8, 2 * TOK, kind=F32)], 2, "meta")(rows, gates)
    return meta


def dispatch(me, own_ids, other_ids, *tokens):
    outs = [shape(8, 2 * TOK, kind=F32)] + [shape(MSG * (len(tokens) // 2), HALF)] * STEPS
    meta, *messages = call(dispatch_kernel, outs, 2 + len(tokens), "dispatch", smem=1)(
        me, own_ids, other_ids, *tokens
    )
    return meta, messages


def send(messages, steps, distance=0):
    if distance:
        routes = [[(j, i) for i, j in near(s)] for s in steps]
        return [to_section(m, distance, route) for m, route in zip(messages, routes)]
    return [lax.ppermute(m, "expert", near(s)) for m, s in zip(messages, steps)]


def join(messages):
    rows = messages[0].shape[0] // MSG * 2 * CAP * len(messages)
    (own,) = call(join_kernel, [shape(rows, D)], len(messages), "join")(*messages)
    return own


def core_sums(parts):
    own, beside, *rest = parts
    n = len(rest) // 2
    from_diagonal = [other_core(piece) for piece in rest[n:]]
    from_beside = other_core(beside)
    sums = [
        call(add_kernel, [shape(*a.shape)], 2, "chip_sum")(a, b)[0]
        for a, b in zip(rest, from_diagonal)
    ]
    return own, from_beside, sums


def pair_sums(steps, own, from_beside, from_across):
    kernel = functools.partial(split_kernel, steps.start * 2 * CAP)
    outs = [shape(MSG, HALF)] * (steps.stop - steps.start)
    return call(kernel, outs, 3, "pair_sum")(own, from_beside, from_across)


def finish(keep, messages, base, meta):
    mine, theirs = call(pick_kernel, [shape(TOK, D)] * 2, 5, "pick")(meta, *messages)
    (out,) = call(final_kernel, [shape(TOK, D)], 4, "final", smem=1)(
        keep, meta, base, mine, other_core(theirs)
    )
    return out


def body(x_fwd, routes_fwd, gates_fwd, x_bwd, grad_bwd, routes_bwd, gates_bwd, gate, up, down):
    x_a, x_b, g_b = x_fwd[0], x_bwd[0], grad_bwd[0]
    gate, up, down = gate[0], up[0], down[0]
    me = lax.axis_index("expert").astype(jnp.int32).reshape(1)
    section = lax.axis_index("pipe").astype(jnp.int32).reshape(1)
    last = lax.axis_size("pipe") - 1
    keep_a, keep_b = (section != 0).astype(jnp.int32), (section != last).astype(jnp.int32)
    same = [(i, i) for i in range(lax.axis_size("expert"))]
    ids_a, ids_b = routes_fwd.reshape(1, TOK), routes_bwd.reshape(1, TOK)
    gates_a, gates_b = gates_fwd.reshape(1, TOK), gates_bwd.reshape(1, TOK)

    other_a, x_a_other = other_core(ids_a), other_core(x_a)
    others_b = other_core(ids_b), other_core(x_b), other_core(g_b)
    me_a = after(me, *others_b)
    meta_a, sent_a = dispatch(me_a, ids_a, other_a, x_a, x_a_other)
    got_a = send(sent_a, range(STEPS))
    late = after(ids_b, got_a[3])
    meta_b, sent_b = dispatch(me, late, others_b[0], x_b, others_b[1], g_b, others_b[2])
    got_b = send(after(sent_b, *got_a[1:]), range(STEPS))

    own_a = join(after(got_a, meta_b))
    across_a = other_chip(own_a)
    rows_a = (own_a, other_core(after(own_a, got_b[3])), across_a, other_core(across_a))
    own_b = join(got_b)
    across_b = other_chip(own_b)
    x_a, g_b, meta_a, meta_b = after((x_a, g_b, meta_a, meta_b), across_a, own_b)
    base_a = to_section(x_a, 1, same)
    base_b = to_section(g_b, -1, same)
    meta_a = to_section(with_gates(meta_a, gates_a), 1, same)
    meta_b = to_section(with_gates(meta_b, gates_b), -1, same)

    outs = [shape(ROWS, D)] * 4
    work = 6 * 384 * D * HID
    parts_a = call(forward_kernel, outs, 7, "expert_fwd", flops=work)(*rows_a, gate, up, down)
    own_a, beside_a, chip_a = core_sums(parts_a)
    across_b = after(across_b, *chip_a, meta_a, meta_b, base_a, base_b)
    rows_b = (own_b, other_core(after(own_b, *chip_a)), across_b, other_core(across_b))
    back_a = other_chip(after(chip_a[0], across_b))
    outs = outs[:2] + [shape(ROWS // 2, D)] * 4
    parts_b = call(backward_kernel, outs, 7, "expert_bwd", flops=2 * work)(*rows_b, gate, up, down)
    own_b, beside_b, chip_b = core_sums(parts_b)
    back_b0 = other_chip(chip_b[0])
    sums_a = pair_sums(slice(0, STEPS), after(own_a, *chip_b), beside_a, back_a)
    back_b1 = other_chip(after(chip_b[1], back_b0, sums_a[0]))
    got_a = send(sums_a[:1], (0,), 1)
    got_a += send(after(sums_a[1:], back_b0, got_a[0]), (1, 2, 3), 1)
    got_b = send(pair_sums(slice(0, 2), own_b, beside_b, back_b0), (0, 1), -1)
    got_b += send(pair_sums(slice(2, 4), own_b, beside_b, back_b1), (2, 3), -1)
    fwd_next = finish(keep_a, got_a, base_a, meta_a)
    bwd_next = finish(keep_b, got_b, base_b, meta_b)
    return fwd_next[None], bwd_next[None]


def solution(mesh):
    rows, cols = P("pipe", "expert", None), P("pipe", None, "expert")
    in_specs = (rows,) * 7 + (cols, cols, rows)
    return jax.shard_map(
        body, mesh=mesh, in_specs=in_specs, out_specs=(rows, rows), check_vma=False
    )
```
